32 devices in a mesh: groups: 2 (over y), row: 4 (over z), col: 2 (over core), seq: 2 (over x).
Axes of the slice: x: 2, y: 2, z: 4, core: 2. Of those that a mesh axis runs over, the one named last changes fastest.
Arguments:
- alignment: bfloat16 [512, 64, 256], P(('groups', 'seq'), ('row', 'col')), parts along dimension 0, may hold values from -16 to 16
- alignment_mask: bfloat16 [512, 64], P(('groups', 'seq'), ('row', 'col')), parts along dimension 0, may hold values from 0 to 1
- norm_gain: float32 [256], replicated, may hold values from 0.1 to 1.9
- norm_bias: float32 [256], replicated, may hold values from -3 to 3
- left_weight: bfloat16 [256, 32], replicated, may hold values from -0.375 to 0.375
- left_bias: float32 [32], replicated, may hold values from -3 to 3
- right_weight: bfloat16 [256, 32], replicated, may hold values from -0.375 to 0.375
- right_bias: float32 [32], replicated, may hold values from -3 to 3
- out_weight: bfloat16 [1024, 128], replicated, may hold values from -0.1875 to 0.1875
- pair_state: bfloat16 [128, 64, 128], P(('groups', 'row'), ('col', 'seq')), parts along dimension 0, may hold values from -6 to 6
Outputs:
- pair_out: bfloat16 [128, 64, 128], P(('groups', 'row'), ('col', 'seq')), parts along dimension 0
The draws below stay inside these ranges and needn't reach their ends.
There are 2 independent parts, one for each index of `groups`. The reference program is written for one: setup_inputs(seed, part) draws one part's arguments, and reference() takes and returns one part's arrays. A program takes and returns all parts, laid end to end along the dimension named above; an argument that names none is the same for every part. Nothing has to cross between parts.
All inputs are finite; a program needn't handle non-finite values.
Results may differ from the reference program's by a relative error of at most 0.0034.
Values may be sent and summed in bfloat16 or wider, within the bound.
A program may use at most 64 MiB of HBM per device.

```python
import math
import jax
import jax.numpy as jnp
from jax import lax

CM = 256
C = 32
CZ = 128
RI_DEV = 16
S = 256
R = 64


def draw_alignment(key, part):
    key = jax.random.fold_in(key, 11)
    key_base = jax.random.fold_in(key, 0)
    key_noise = jax.random.fold_in(key, 1)
    key_chan = jax.random.fold_in(key, 2)
    key_holes = jax.random.fold_in(key, 4)
    base = jax.random.normal(key_base, (R, CM), jnp.float32)
    noise = 0.8 * jax.random.normal(key_noise, (S, R, CM), jnp.float32)
    chan_scale = jnp.exp(jax.random.uniform(key_chan, (CM,), jnp.float32, 0.0, math.log(10.0))) * 0.4
    whole = (base[None, :, :] + noise) * chan_scale
    holes = jax.random.randint(key_holes, (S, R, 1), 0, 64) == 0
    whole = jnp.where(holes, 0.0, whole)
    return jnp.clip(whole, -16.0, 16.0).astype(jnp.bfloat16)


def draw_alignment_mask(key, part):
    key = jax.random.fold_in(key, 12)
    key_levels, key_weight = jax.random.split(key, 2)
    levels = jax.random.randint(key_levels, (S, R), 0, 3 * S)
    seq_index = jnp.arange(S, dtype=jnp.int32)[:, None]
    weights = jax.random.uniform(key_weight, (S, R), jnp.float32, 0.25, 1.0)
    values = jnp.where(levels < S + 2 * seq_index, weights, 0.0)
    values = jnp.where(seq_index == 0, 1.0, values)
    return values.astype(jnp.bfloat16)


def shard_levels(own_key, shape, cuts, low, top_value):
    loudness = 1.0
    for dim, parts in cuts:
        draws = jax.random.uniform(jax.random.fold_in(jax.random.fold_in(own_key, 6), dim), (parts,), jnp.float32, low / len(cuts), top_value / len(cuts))
        loudness = loudness * jnp.repeat(jnp.exp(draws), shape[dim] // parts).reshape((-1,) + (1,) * (len(shape) - 1 - dim))
    return loudness


def scatter_about(own_key, dims, width, most, cuts=(), kind=jnp.bfloat16):
    gain = shard_levels(own_key, dims, cuts, -0.22, 0.18) if cuts else 1.0
    values = jax.random.normal(own_key, dims, jnp.float32) * width * gain
    return jnp.minimum(jnp.maximum(values, -most), most).astype(kind)


def setup_inputs(seed: int = 0, part: int = 0) -> dict:
    splits = jax.random.split(jax.random.key(seed), 11)
    part_keys = jax.random.split(jax.random.fold_in(splits[10], part), 11)
    alignment = draw_alignment(jax.random.fold_in(jax.random.fold_in(splits[10], part), 71), part)
    alignment_mask = draw_alignment_mask(jax.random.fold_in(jax.random.fold_in(splits[10], part), 71), part)
    norm_gain = jnp.clip(1.0 + 0.18 * jax.random.normal(splits[2], (CM,), jnp.float32), 0.1, 1.9)
    norm_bias = scatter_about(splits[3], (CM,), 0.5, 3.0, (), jnp.float32)
    left_weight = scatter_about(splits[4], (CM, C), CM ** -0.5, 0.375)
    left_bias = scatter_about(splits[5], (C,), 0.5, 3.0, (), jnp.float32)
    right_weight = scatter_about(splits[6], (CM, C), CM ** -0.5, 0.375)
    right_bias = scatter_about(splits[7], (C,), 0.5, 3.0, (), jnp.float32)
    out_weight = scatter_about(splits[8], (C * C, CZ), (C * C) ** -0.5, 0.1875)
    pair_state = scatter_about(part_keys[9], (R, R, CZ), 1.0, 6.0, ((0, 4), (1, 4)))
    return dict(alignment=alignment, alignment_mask=alignment_mask, norm_gain=norm_gain, norm_bias=norm_bias, left_weight=left_weight, left_bias=left_bias, right_weight=right_weight, right_bias=right_bias, out_weight=out_weight, pair_state=pair_state)


def reference(alignment, alignment_mask, norm_gain, norm_bias, left_weight, left_bias, right_weight, right_bias, out_weight, pair_state):
    values = alignment.astype(jnp.float32)
    center = lax.optimization_barrier(jnp.mean(values, axis=-1, keepdims=True))
    spread = lax.optimization_barrier(jnp.mean(jnp.square(values - center), axis=-1, keepdims=True))
    normed = ((values - center) * lax.rsqrt(spread + 1e-05) * norm_gain + norm_bias).astype(jnp.bfloat16)
    flat_rows = normed.reshape(S * R, CM)
    present = alignment_mask.astype(jnp.float32)
    left_proj = ((jnp.dot(flat_rows, left_weight, preferred_element_type=jnp.float32).reshape(S, R, C) + left_bias) * present[:, :, None]).astype(jnp.bfloat16)
    right_proj = ((jnp.dot(flat_rows, right_weight, preferred_element_type=jnp.float32).reshape(S, R, C) + right_bias) * present[:, :, None]).astype(jnp.bfloat16)
    weight_flat = out_weight.astype(jnp.float32)
    blocks = R // RI_DEV
    left_blocks = left_proj.reshape(S, blocks, RI_DEV, C).transpose(1, 0, 2, 3)
    mask_blocks = present.reshape(S, blocks, RI_DEV).transpose(1, 0, 2)
    pair_blocks = pair_state.reshape(blocks, RI_DEV, R, CZ)
    right_wide = right_proj.astype(jnp.float32)

    def one_block(inputs):
        left_block, mask_block, pair_block = inputs
        outer = jnp.einsum('sic,sje->ijce', left_block.astype(jnp.float32), right_wide).reshape(RI_DEV * R, C * C)
        update = jnp.dot(outer, weight_flat, precision=lax.Precision.HIGHEST, preferred_element_type=jnp.float32).reshape(RI_DEV, R, CZ)
        counts = jnp.einsum('si,sj->ij', mask_block, present)
        return (pair_block.astype(jnp.float32) + update / (counts[:, :, None] + 0.001)).astype(jnp.bfloat16)
    result = lax.map(one_block, (left_blocks, mask_blocks, pair_blocks))
    return result.reshape(R, R, CZ)
```

```python
import functools

import jax
import jax.numpy as jnp
from jax import lax
from jax.experimental import pallas as pl
from jax.experimental.pallas import tpu as pltpu
from jax.sharding import PartitionSpec as P

MESH = pl.DeviceIdType.MESH
F32 = jnp.float32
BF16 = jnp.bfloat16
ROW_TILE = 16
LANES = 128


def dot_nt(a, b):
    return lax.dot_general(a, b, (((1,), (1,)), ((), ())), preferred_element_type=F32)


def kernel(
    sizes,
    x_ref, mask_ref, gain_ref, bias_ref, wl_ref, bl_ref, wr_ref, br_ref, wout_ref, pair_ref,
    out_ref,
    normed, shuffle, wide, own_right, left_buf, right_buf, spread, big_w, part, part_in,
    count, count_in,
    send_left, recv_left, send_right, recv_right, send_part, recv_part, send_count, recv_count,
):
    n_row, n_col, n_seq = sizes
    seqs, res, chans = x_ref.shape
    ch = wl_ref.shape[1]
    rows_i, cols_j, pair_ch = pair_ref.shape
    block = res * ch
    half = n_row // n_col
    chip_res = res * n_col
    chunks = cols_j // chip_res
    groups = LANES // ch
    ig_count = rows_i // groups
    row, col, seq = lax.axis_index("row"), lax.axis_index("col"), lax.axis_index("seq")
    dest_col = row // half
    my_slot = (row % half) * n_col + col

    barrier = pltpu.get_barrier_semaphore()
    for k in range(1, n_row * n_col):
        flat = (row * n_col + col + k) % (n_row * n_col)
        pl.semaphore_signal(
            barrier, inc=1, device_id={"row": flat // n_col, "col": flat % n_col},
            device_id_type=MESH,
        )
    for k in range(1, n_seq):
        pl.semaphore_signal(
            barrier, inc=1, device_id={"seq": (seq + k) % n_seq}, device_id_type=MESH
        )

    gain, shift = gain_ref[...], bias_ref[...]
    step = 16
    for first in range(0, seqs, step):
        values = x_ref[first : first + step].astype(F32).reshape(step * res, chans)
        center = jnp.mean(values, axis=-1, keepdims=True)
        values = values - center
        var = jnp.mean(values * values, axis=-1, keepdims=True)
        values = values * lax.rsqrt(var + 1e-05) * gain + shift
        for lane in range(0, chans, LANES):
            normed[lane // LANES, first * res : (first + step) * res, :] = values[
                :, lane : lane + LANES
            ]

    weight_t = jnp.concatenate([wl_ref[...], wr_ref[...]], axis=1).astype(F32).T.astype(BF16)
    bias_t = jnp.concatenate([bl_ref[...], br_ref[...]], axis=1)
    bias_t = jnp.broadcast_to(bias_t, (8, 2 * ch)).T[:, 0:1]
    mask_t = mask_ref[...].astype(F32).T
    for r in range(res):
        picked = jnp.concatenate(
            [normed[h, pl.ds(r, seqs, stride=res), :] for h in range(chans // LANES)], axis=1
        ).astype(BF16)
        proj = (dot_nt(weight_t, picked) + bias_t) * mask_t[r : r + 1, :]
        left_buf[col, r * ch : (r + 1) * ch, :] = proj[:ch].astype(BF16)
        shuffle[pl.ds(r, ch, stride=res), :] = proj[ch:]
    mask_rows = jnp.concatenate([mask_t, jnp.zeros_like(mask_t)], axis=0)[:ROW_TILE].astype(BF16)
    left_buf[col, block : block + ROW_TILE, :] = mask_rows
    own_right[0:block, :] = shuffle[...].astype(BF16)
    own_right[block : block + ROW_TILE, :] = mask_rows

    pl.semaphore_wait(barrier, n_row * n_col - 1 + n_seq - 1)

    def left_copy(k):
        return pltpu.make_async_remote_copy(
            src_ref=left_buf.at[col], dst_ref=left_buf.at[col], send_sem=send_left.at[k],
            recv_sem=recv_left.at[col], device_id={"col": (col + k) % n_col}, device_id_type=MESH,
        )

    def left_arrival(k):
        other = (col + k) % n_col
        return pltpu.make_async_remote_copy(
            src_ref=left_buf.at[other], dst_ref=left_buf.at[other], send_sem=send_left.at[k],
            recv_sem=recv_left.at[other], device_id={"col": other}, device_id_type=MESH,
        )

    def right_copy(k):
        return pltpu.make_async_remote_copy(
            src_ref=own_right, dst_ref=right_buf.at[my_slot], send_sem=send_right.at[k],
            recv_sem=recv_right.at[my_slot],
            device_id={"row": (row + k) % n_row, "col": dest_col}, device_id_type=MESH,
        )

    def right_wait(slot):
        pltpu.make_async_copy(own_right, right_buf.at[slot], recv_right.at[slot]).wait()

    for k in range(1, n_row):
        right_copy(k).start()

    @pl.when(dest_col != col)
    def _():
        right_copy(0).start()

    @pl.when(dest_col == col)
    def _():
        pltpu.make_async_copy(own_right, right_buf.at[my_slot], recv_right.at[my_slot]).start()

    for k in range(1, n_col):
        left_copy(k).start()

    wide[...] = wout_ref[...].astype(F32)
    big_w[...] = jnp.zeros_like(big_w)
    for e in range(ch):
        piece = wide[pl.ds(e, ch, stride=ch), :].astype(BF16)
        for g in range(groups):
            start = e * LANES + g * ch
            big_w[start : start + ch, g * pair_ch : (g + 1) * pair_ch] = piece

    for k in range(1, n_col):
        left_arrival(k).wait_recv()
    left = jnp.concatenate([left_buf[n, 0:block, :] for n in range(n_col)], axis=0)
    left_mask = jnp.concatenate(
        [left_buf[n, block : block + ROW_TILE, :].astype(F32)[:res] for n in range(n_col)], axis=0
    )
    left_mask = jnp.concatenate(
        [left_mask, jnp.zeros((LANES - rows_i, seqs), F32)], axis=0
    ).astype(BF16)

    def chunk_update(chunk):
        outers, masks = [], []
        for n in range(n_col):
            slot = chunk * n_col + n
            right_wait(slot)
            outers.append(dot_nt(right_buf[slot, 0:block, :], left))
            masks.append(right_buf[slot, block : block + ROW_TILE, :].astype(F32)[:res])
        half_rows = ig_count * chip_res
        for e in range(ch):
            both = jnp.concatenate([o[e * res : (e + 1) * res, :] for o in outers], axis=0)
            high = both.astype(BF16)
            low = (both - high.astype(F32)).astype(BF16)
            for ig in range(ig_count):
                rows = slice(ig * chip_res, (ig + 1) * chip_res)
                low_rows = slice(half_rows + ig * chip_res, half_rows + (ig + 1) * chip_res)
                lanes = slice(e * LANES, (e + 1) * LANES)
                spread[rows, lanes] = high[:, ig * LANES : (ig + 1) * LANES]
                spread[low_rows, lanes] = low[:, ig * LANES : (ig + 1) * LANES]
        product = jnp.dot(spread[...], big_w[...], preferred_element_type=F32)
        product = product[:half_rows] + product[half_rows:]
        right_mask = jnp.concatenate(masks, axis=0).astype(BF16)
        return product, dot_nt(right_mask, left_mask)

    def tile(product, i):
        ig, g = i // groups, i % groups
        return product[
            ig * chip_res : (ig + 1) * chip_res, g * pair_ch : (g + 1) * pair_ch
        ]

    def part_copy(k):
        return pltpu.make_async_remote_copy(
            src_ref=part.at[k], dst_ref=part_in.at[k], send_sem=send_part.at[k],
            recv_sem=recv_part.at[k], device_id={"seq": (seq + k) % n_seq}, device_id_type=MESH,
        )

    def count_copy(k):
        return pltpu.make_async_remote_copy(
            src_ref=count.at[k], dst_ref=count_in.at[k], send_sem=send_count.at[k],
            recv_sem=recv_count.at[k], device_id={"seq": (seq + k) % n_seq}, device_id_type=MESH,
        )

    for k in range(1, n_seq):
        for piece in range(chunks):
            product, counts = chunk_update(((seq + k) % n_seq) * chunks + piece)
            place = slice(piece * chip_res, (piece + 1) * chip_res)
            for i in range(rows_i):
                part[k, i, place, :] = tile(product, i).astype(BF16)
            count[k, place, :] = counts
        part_copy(k).start()
        count_copy(k).start()

    for piece in range(chunks):
        product, counts = chunk_update(seq * chunks + piece)
        place = slice(piece * chip_res, (piece + 1) * chip_res)
        if piece == 0:
            for k in range(1, n_seq):
                part_copy(k).wait_recv()
                count_copy(k).wait_recv()
        for k in range(1, n_seq):
            counts = counts + count_in[k, place, :]
        scale = 1.0 / (counts + 0.001)
        for i in range(rows_i):
            total = tile(product, i)
            for k in range(1, n_seq):
                total = total + part_in[k, i, place, :].astype(F32)
            out_ref[i, place, :] = (
                pair_ref[i, place, :].astype(F32) + total * scale[:, i : i + 1]
            ).astype(BF16)

    for k in range(1, n_row):
        right_copy(k).wait_send()

    @pl.when(dest_col != col)
    def _():
        right_copy(0).wait_send()

    for k in range(1, n_col):
        left_copy(k).wait_send()
    for k in range(1, n_seq):
        part_copy(k).wait_send()
        count_copy(k).wait_send()


def on_device(
    sizes,
    alignment, alignment_mask, norm_gain, norm_bias, left_weight, left_bias, right_weight,
    right_bias, out_weight, pair_state,
):
    n_row, n_col, n_seq = sizes
    seqs, res, chans = alignment.shape
    ch = left_weight.shape[1]
    rows_i, cols_j, pair_ch = pair_state.shape
    block = res * ch + ROW_TILE
    groups = LANES // ch
    dma = pltpu.SemaphoreType.DMA
    vmem = pl.BlockSpec(memory_space=pltpu.VMEM)
    return pl.pallas_call(
        functools.partial(kernel, sizes),
        out_shape=jax.ShapeDtypeStruct(pair_state.shape, BF16),
        in_specs=[vmem] * 10,
        out_specs=vmem,
        scratch_shapes=[
            pltpu.VMEM((chans // LANES, seqs * res, LANES), F32),
            pltpu.VMEM((res * ch, seqs), F32),
            pltpu.VMEM(out_weight.shape, F32),
            pltpu.VMEM((block, seqs), BF16),
            pltpu.VMEM((n_col, block, seqs), BF16),
            pltpu.VMEM((n_row, block, seqs), BF16),
            pltpu.VMEM((2 * (rows_i // groups) * res * n_col, ch * LANES), BF16),
            pltpu.VMEM((ch * LANES, groups * pair_ch), BF16),
            pltpu.VMEM((n_seq, rows_i, cols_j, pair_ch), BF16),
            pltpu.VMEM((n_seq, rows_i, cols_j, pair_ch), BF16),
            pltpu.VMEM((n_seq, cols_j, LANES), F32),
            pltpu.VMEM((n_seq, cols_j, LANES), F32),
            dma((n_col,)), dma((n_col,)), dma((n_row,)), dma((n_row,)),
            dma((n_seq,)), dma((n_seq,)), dma((n_seq,)), dma((n_seq,)),
        ],
        compiler_params=pltpu.CompilerParams(
            collective_id=0, has_side_effects=True, vmem_limit_bytes=40 * 1024 * 1024
        ),
    )(
        alignment, alignment_mask, norm_gain.reshape(1, chans), norm_bias.reshape(1, chans),
        left_weight, left_bias.reshape(1, ch), right_weight, right_bias.reshape(1, ch),
        out_weight, pair_state,
    )


def solution(mesh):
    sizes = tuple(mesh.shape[name] for name in ("row", "col", "seq"))
    in_specs = (
        P(("groups", "seq"), ("row", "col"), None),
        P(("groups", "seq"), ("row", "col")),
        P(), P(), P(), P(), P(), P(), P(),
        P(("groups", "row"), ("col", "seq"), None),
    )
    return jax.shard_map(
        functools.partial(on_device, sizes),
        mesh=mesh,
        in_specs=in_specs,
        out_specs=P(("groups", "row"), ("col", "seq"), None),
        check_vma=False,
    )
```

```python
import functools

import jax
import jax.numpy as jnp
from jax import lax
from jax.experimental import pallas as pl
from jax.experimental.pallas import tpu as pltpu
from jax.sharding import PartitionSpec as P

MESH = pl.DeviceIdType.MESH
F32 = jnp.float32
BF16 = jnp.bfloat16
ROW_TILE = 16
LANES = 128
X_PARTS = 4


def dot_nt(a, b):
    return lax.dot_general(a, b, (((1,), (1,)), ((), ())), preferred_element_type=F32)


def kernel(
    sizes,
    x_hbm, mask_hbm, gain_hbm, bias_hbm, wl_hbm, bl_hbm, wr_hbm, br_hbm, wout_hbm, pair_hbm,
    out_ref,
    x_ref, mask_ref, gain_ref, bias_ref, weight_ref, bl_ref, br_ref, wout_ref, pair_ref,
    normed, shuffle, wide, own_right, left_buf, right_buf, spread, big_w,
    in_sem, send_left, recv_left, send_right, recv_right,
):
    n_row, n_col, n_seq = sizes
    seqs, res, chans = x_ref.shape
    ch = wl_hbm.shape[0]
    rows_i, cols_j, pair_ch = pair_ref.shape
    block = res * ch
    chip_res = res * n_col
    chunks = cols_j // chip_res
    cores = n_col * n_seq
    groups = LANES // ch
    ig_count = rows_i // groups
    row, col, seq = lax.axis_index("row"), lax.axis_index("col"), lax.axis_index("seq")
    here = col * n_seq + seq
    dest_col, dest_seq = row // chunks // n_seq, row // chunks % n_seq
    stays = dest_col * n_seq + dest_seq == here
    my_chunk = row % chunks

    copies = [
        pltpu.make_async_copy(mask_hbm, mask_ref, in_sem.at[0]),
        pltpu.make_async_copy(gain_hbm, gain_ref, in_sem.at[1]),
        pltpu.make_async_copy(bias_hbm, bias_ref, in_sem.at[2]),
        pltpu.make_async_copy(wl_hbm, weight_ref.at[0:ch], in_sem.at[3]),
        pltpu.make_async_copy(wr_hbm, weight_ref.at[ch : 2 * ch], in_sem.at[4]),
        pltpu.make_async_copy(bl_hbm, bl_ref, in_sem.at[5]),
        pltpu.make_async_copy(br_hbm, br_ref, in_sem.at[6]),
    ]
    late = [
        pltpu.make_async_copy(wout_hbm, wout_ref, in_sem.at[7]),
        pltpu.make_async_copy(pair_hbm, pair_ref, in_sem.at[8]),
    ]
    part = seqs // X_PARTS
    x_copies = [
        pltpu.make_async_copy(
            x_hbm.at[n * part : (n + 1) * part], x_ref.at[n * part : (n + 1) * part],
            in_sem.at[9 + n],
        )
        for n in range(X_PARTS)
    ]
    for copy in x_copies[:1] + copies + x_copies[1:] + late:
        copy.start()

    barrier = pltpu.get_barrier_semaphore()
    for piece in range(chunks):
        source = here * chunks + piece
        for n in range(cores):
            @pl.when((source != row) | (here != n))
            def _():
                pl.semaphore_signal(
                    barrier, inc=1, device_id_type=MESH,
                    device_id={"row": source, "col": n // n_seq, "seq": n % n_seq},
                )
    for k in range(1, cores):
        other = (here + k) % cores
        pl.semaphore_signal(
            barrier, inc=1, device_id={"col": other // n_seq, "seq": other % n_seq},
            device_id_type=MESH,
        )

    for copy in copies:
        copy.wait()
    gain, shift = gain_ref[...], bias_ref[...]
    step = 16
    for first in range(0, seqs, step):
        if first % part == 0:
            x_copies[first // part].wait()
        values = x_ref[first : first + step].astype(F32).reshape(step * res, chans)
        center = jnp.mean(values, axis=-1, keepdims=True)
        values = values - center
        var = jnp.mean(values * values, axis=-1, keepdims=True)
        values = values * lax.rsqrt(var + 1e-05) * gain + shift
        for lane in range(0, chans, LANES):
            normed[lane // LANES, first * res : (first + step) * res, :] = values[
                :, lane : lane + LANES
            ]

    weight_t = weight_ref[...]
    bias_t = jnp.concatenate([bl_ref[...], br_ref[...]], axis=1)
    bias_t = jnp.broadcast_to(bias_t, (8, 2 * ch)).T[:, 0:1]
    mask_t = mask_ref[...].astype(F32)
    for r in range(res):
        picked = jnp.concatenate(
            [normed[h, pl.ds(r, seqs, stride=res), :] for h in range(chans // LANES)], axis=1
        ).astype(BF16)
        proj = (dot_nt(weight_t, picked) + bias_t) * mask_t[r : r + 1, :]
        left_buf[col, seq, r * ch : (r + 1) * ch, :] = proj[:ch].astype(BF16)
        shuffle[pl.ds(r, ch, stride=res), :] = proj[ch:]
    mask_rows = jnp.concatenate([mask_t, jnp.zeros_like(mask_t)], axis=0)[:ROW_TILE].astype(BF16)
    left_buf[col, seq, block : block + ROW_TILE, :] = mask_rows
    own_right[0:block, :] = shuffle[...].astype(BF16)
    own_right[block : block + ROW_TILE, :] = mask_rows

    def left_copy(k):
        other = (here + k) % cores
        return pltpu.make_async_remote_copy(
            src_ref=left_buf.at[col, seq], dst_ref=left_buf.at[col, seq],
            send_sem=send_left.at[k], recv_sem=recv_left.at[col, seq],
            device_id={"col": other // n_seq, "seq": other % n_seq}, device_id_type=MESH,
        )

    def right_copy(k):
        return pltpu.make_async_remote_copy(
            src_ref=own_right, dst_ref=right_buf.at[my_chunk, col, seq],
            send_sem=send_right.at[k], recv_sem=recv_right.at[my_chunk, col, seq],
            device_id={"row": (row + k) % n_row, "col": dest_col, "seq": dest_seq},
            device_id_type=MESH,
        )

    def right_local():
        return pltpu.make_async_copy(
            own_right, right_buf.at[my_chunk, col, seq], recv_right.at[my_chunk, col, seq]
        )

    @pl.when(stays)
    def _():
        right_local().start()
        pl.semaphore_wait(barrier, n_row - 1 + cores - 1)

    @pl.when(jnp.logical_not(stays))
    def _():
        pl.semaphore_wait(barrier, n_row + cores - 1)
        right_copy(0).start()

    for k in range(1, n_row):
        right_copy(k).start()
    for k in range(1, cores):
        left_copy(k).start()

    for copy in late:
        copy.wait()
    wide[...] = wout_ref[...].astype(F32)
    big_w[...] = jnp.zeros_like(big_w)
    for e in range(ch):
        piece = wide[pl.ds(e, ch, stride=ch), :].astype(BF16)
        for g in range(groups):
            start = e * LANES + g * ch
            big_w[start : start + ch, g * pair_ch : (g + 1) * pair_ch] = piece

    for k in range(1, cores):
        other = (here + k) % cores
        slot = (other // n_seq, other % n_seq)
        pltpu.make_async_copy(own_right, left_buf.at[slot], recv_left.at[slot]).wait()

    def both_seqs(buf, at, rows):
        return jnp.concatenate([buf[(*at, q, rows)] for q in range(n_seq)], axis=1)

    def masks(buf, at, rows_to):
        found = [
            both_seqs(buf, (*at, n), slice(block, block + ROW_TILE)).astype(F32)[:res]
            for n in range(n_col)
        ]
        if rows_to > chip_res:
            found.append(jnp.zeros((rows_to - chip_res, n_seq * seqs), F32))
        return jnp.concatenate(found, axis=0).astype(BF16)

    left = jnp.concatenate(
        [both_seqs(left_buf, (n,), slice(0, block)) for n in range(n_col)], axis=0
    )
    left_mask = masks(left_buf, (), LANES)
    half_rows = ig_count * chip_res

    for piece in range(chunks):
        outers = []
        for n in range(n_col):
            for q in range(n_seq):
                pltpu.make_async_copy(
                    own_right, right_buf.at[piece, n, q], recv_right.at[piece, n, q]
                ).wait()
            outers.append(dot_nt(both_seqs(right_buf, (piece, n), slice(0, block)), left))
        for e in range(ch):
            both = jnp.concatenate([o[e * res : (e + 1) * res, :] for o in outers], axis=0)
            high = both.astype(BF16)
            low = (both - high.astype(F32)).astype(BF16)
            for ig in range(ig_count):
                rows = slice(ig * chip_res, (ig + 1) * chip_res)
                low_rows = slice(half_rows + ig * chip_res, half_rows + (ig + 1) * chip_res)
                lanes = slice(e * LANES, (e + 1) * LANES)
                spread[rows, lanes] = high[:, ig * LANES : (ig + 1) * LANES]
                spread[low_rows, lanes] = low[:, ig * LANES : (ig + 1) * LANES]
        product = jnp.dot(spread[...], big_w[...], preferred_element_type=F32)
        product = product[:half_rows] + product[half_rows:]
        counts = dot_nt(masks(right_buf, (piece,), chip_res), left_mask)
        scale = 1.0 / (counts + 0.001)
        place = slice(piece * chip_res, (piece + 1) * chip_res)
        for i in range(rows_i):
            ig, g = i // groups, i % groups
            update = product[
                ig * chip_res : (ig + 1) * chip_res, g * pair_ch : (g + 1) * pair_ch
            ]
            out_ref[i, place, :] = (
                pair_ref[i, place, :].astype(F32) + update * scale[:, i : i + 1]
            ).astype(BF16)

    for k in range(1, n_row):
        right_copy(k).wait_send()

    @pl.when(jnp.logical_not(stays))
    def _():
        right_copy(0).wait_send()

    for k in range(1, cores):
        left_copy(k).wait_send()


def on_device(
    sizes,
    alignment, alignment_mask, norm_gain, norm_bias, left_weight, left_bias, right_weight,
    right_bias, out_weight, pair_state,
):
    n_row, n_col, n_seq = sizes
    seqs, res, chans = alignment.shape
    ch = left_weight.shape[1]
    rows_i, cols_j, pair_ch = pair_state.shape
    block = res * ch + ROW_TILE
    chunks = cols_j // (res * n_col)
    groups = LANES // ch
    dma = pltpu.SemaphoreType.DMA
    return pl.pallas_call(
        functools.partial(kernel, sizes),
        out_shape=jax.ShapeDtypeStruct(pair_state.shape, BF16),
        in_specs=[pl.BlockSpec(memory_space=pl.ANY)] * 10,
        out_specs=pl.BlockSpec(memory_space=pltpu.VMEM),
        scratch_shapes=[
            pltpu.VMEM(alignment.shape, BF16),
            pltpu.VMEM((res, seqs), BF16),
            pltpu.VMEM((1, chans), F32),
            pltpu.VMEM((1, chans), F32),
            pltpu.VMEM((2 * ch, chans), BF16),
            pltpu.VMEM((1, ch), F32),
            pltpu.VMEM((1, ch), F32),
            pltpu.VMEM(out_weight.shape, BF16),
            pltpu.VMEM(pair_state.shape, BF16),
            pltpu.VMEM((chans // LANES, seqs * res, LANES), F32),
            pltpu.VMEM((res * ch, seqs), F32),
            pltpu.VMEM(out_weight.shape, F32),
            pltpu.VMEM((block, seqs), BF16),
            pltpu.VMEM((n_col, n_seq, block, seqs), BF16),
            pltpu.VMEM((chunks, n_col, n_seq, block, seqs), BF16),
            pltpu.VMEM((2 * (rows_i // groups) * res * n_col, ch * LANES), BF16),
            pltpu.VMEM((ch * LANES, groups * pair_ch), BF16),
            dma((9 + X_PARTS,)), dma((n_col * n_seq,)), dma((n_col, n_seq)), dma((n_row,)),
            dma((chunks, n_col, n_seq)),
        ],
        compiler_params=pltpu.CompilerParams(
            collective_id=0, has_side_effects=True, vmem_limit_bytes=56 * 1024 * 1024
        ),
    )(
        alignment, alignment_mask.T, norm_gain.reshape(1, chans), norm_bias.reshape(1, chans),
        left_weight.T, left_bias.reshape(1, ch), right_weight.T, right_bias.reshape(1, ch),
        out_weight, pair_state,
    )


def solution(mesh):
    sizes = tuple(mesh.shape[name] for name in ("row", "col", "seq"))
    in_specs = (
        P(("groups", "seq"), ("row", "col"), None),
        P(("groups", "seq"), ("row", "col")),
        P(), P(), P(), P(), P(), P(), P(),
        P(("groups", "row"), ("col", "seq"), None),
    )
    return jax.shard_map(
        functools.partial(on_device, sizes),
        mesh=mesh,
        in_specs=in_specs,
        out_specs=P(("groups", "row"), ("col", "seq"), None),
        check_vma=False,
    )
```

```python
import functools

import jax
import jax.numpy as jnp
from jax import lax
from jax.experimental import pallas as pl
from jax.experimental.pallas import tpu as pltpu
from jax.sharding import PartitionSpec as P

MESH = pl.DeviceIdType.MESH
F32 = jnp.float32
BF16 = jnp.bfloat16
ROW_TILE = 16
LANES = 128
X_PARTS = 4


def dot_nt(a, b):
    return lax.dot_general(a, b, (((1,), (1,)), ((), ())), preferred_element_type=F32)


def kernel(
    sizes,
    x_hbm, mask_hbm, gain_hbm, bias_hbm, wl_hbm, bl_hbm, wr_hbm, br_hbm, wout_hbm, pair_hbm,
    out_ref,
    x_ref, mask_ref, gain_ref, bias_ref, weight_ref, bl_ref, br_ref, wout_ref, pair_ref,
    normed, shuffle, wide, own_right, left_buf, right_buf, spread, big_w,
    in_sem, send_left, recv_left, send_right, recv_right, send_seq,
):
    n_row, n_col, n_seq = sizes
    seqs, res, chans = x_ref.shape
    ch = wl_hbm.shape[0]
    rows_i, cols_j, pair_ch = pair_ref.shape
    block = res * ch
    chip_res = res * n_col
    chunks = cols_j // chip_res
    cores = n_col * n_seq
    groups = LANES // ch
    ig_count = rows_i // groups
    row, col, seq = lax.axis_index("row"), lax.axis_index("col"), lax.axis_index("seq")
    here = col * n_seq + seq
    dest_col, dest_seq = row // chunks // n_seq, row // chunks % n_seq
    stays = dest_col * n_seq + dest_seq == here
    my_chunk = row % chunks

    copies = [
        pltpu.make_async_copy(mask_hbm, mask_ref, in_sem.at[0]),
        pltpu.make_async_copy(gain_hbm, gain_ref, in_sem.at[1]),
        pltpu.make_async_copy(bias_hbm, bias_ref, in_sem.at[2]),
        pltpu.make_async_copy(wl_hbm, weight_ref.at[0:ch], in_sem.at[3]),
        pltpu.make_async_copy(wr_hbm, weight_ref.at[ch : 2 * ch], in_sem.at[4]),
        pltpu.make_async_copy(bl_hbm, bl_ref, in_sem.at[5]),
        pltpu.make_async_copy(br_hbm, br_ref, in_sem.at[6]),
    ]
    late = [
        pltpu.make_async_copy(wout_hbm, wout_ref, in_sem.at[7]),
        pltpu.make_async_copy(pair_hbm, pair_ref, in_sem.at[8]),
    ]
    part = seqs // X_PARTS
    x_copies = [
        pltpu.make_async_copy(
            x_hbm.at[n * part : (n + 1) * part], x_ref.at[n * part : (n + 1) * part],
            in_sem.at[9 + n],
        )
        for n in range(X_PARTS)
    ]
    for copy in x_copies[:1] + copies + x_copies[1:] + late:
        copy.start()

    barrier = pltpu.get_barrier_semaphore()
    for piece in range(chunks):
        source = here * chunks + piece
        for n in range(cores):
            @pl.when((source != row) | (here != n))
            def _():
                pl.semaphore_signal(
                    barrier, inc=1, device_id_type=MESH,
                    device_id={"row": source, "col": n // n_seq, "seq": n % n_seq},
                )
    near = n_col - 1 + n_seq - 1
    for n in range(1, n_col):
        pl.semaphore_signal(
            barrier, inc=1, device_id={"col": (col + n) % n_col}, device_id_type=MESH
        )
    for k in range(1, n_seq):
        pl.semaphore_signal(
            barrier, inc=1, device_id={"seq": (seq + k) % n_seq}, device_id_type=MESH
        )

    for copy in copies:
        copy.wait()
    gain, shift = gain_ref[...], bias_ref[...]
    step = 16
    for first in range(0, seqs, step):
        if first % part == 0:
            x_copies[first // part].wait()
        values = x_ref[first : first + step].astype(F32).reshape(step * res, chans)
        center = jnp.mean(values, axis=-1, keepdims=True)
        values = values - center
        var = jnp.mean(values * values, axis=-1, keepdims=True)
        values = values * lax.rsqrt(var + 1e-05) * gain + shift
        for lane in range(0, chans, LANES):
            normed[lane // LANES, first * res : (first + step) * res, :] = values[
                :, lane : lane + LANES
            ]

    weight_t = weight_ref[...]
    bias_t = jnp.concatenate([bl_ref[...], br_ref[...]], axis=1)
    bias_t = jnp.broadcast_to(bias_t, (8, 2 * ch)).T[:, 0:1]
    mask_t = mask_ref[...].astype(F32)
    for r in range(res):
        picked = jnp.concatenate(
            [normed[h, pl.ds(r, seqs, stride=res), :] for h in range(chans // LANES)], axis=1
        ).astype(BF16)
        proj = (dot_nt(weight_t, picked) + bias_t) * mask_t[r : r + 1, :]
        left_buf[col, seq, r * ch : (r + 1) * ch, :] = proj[:ch].astype(BF16)
        shuffle[pl.ds(r, ch, stride=res), :] = proj[ch:]
    mask_rows = jnp.concatenate([mask_t, jnp.zeros_like(mask_t)], axis=0)[:ROW_TILE].astype(BF16)
    left_buf[col, seq, block : block + ROW_TILE, :] = mask_rows
    own_right[0:block, :] = shuffle[...].astype(BF16)
    own_right[block : block + ROW_TILE, :] = mask_rows

    def to_seq(k):
        return pltpu.make_async_remote_copy(
            src_ref=left_buf.at[col, seq], dst_ref=left_buf.at[col, seq],
            send_sem=send_seq.at[k], recv_sem=recv_left.at[col, seq],
            device_id={"seq": (seq + k) % n_seq}, device_id_type=MESH,
        )

    def to_core(n, q):
        return pltpu.make_async_remote_copy(
            src_ref=left_buf.at[col, q], dst_ref=left_buf.at[col, q],
            send_sem=send_left.at[n, q], recv_sem=recv_left.at[col, q],
            device_id={"col": (col + n) % n_col}, device_id_type=MESH,
        )

    def left_wait(n, q):
        pltpu.make_async_copy(own_right, left_buf.at[n, q], recv_left.at[n, q]).wait()

    def right_copy(k):
        return pltpu.make_async_remote_copy(
            src_ref=own_right, dst_ref=right_buf.at[my_chunk, col, seq],
            send_sem=send_right.at[k], recv_sem=recv_right.at[my_chunk, col, seq],
            device_id={"row": (row + k) % n_row, "col": dest_col, "seq": dest_seq},
            device_id_type=MESH,
        )

    def right_local():
        return pltpu.make_async_copy(
            own_right, right_buf.at[my_chunk, col, seq], recv_right.at[my_chunk, col, seq]
        )

    @pl.when(stays)
    def _():
        right_local().start()
        pl.semaphore_wait(barrier, n_row - 1 + near)

    @pl.when(jnp.logical_not(stays))
    def _():
        pl.semaphore_wait(barrier, n_row + near)
        right_copy(0).start()

    for n in range(1, n_col):
        to_core(n, seq).start()
    for k in range(1, n_seq):
        to_seq(k).start()
    for k in range(1, n_row):
        right_copy(k).start()

    for copy in late:
        copy.wait()
    wide[...] = wout_ref[...].astype(F32)
    big_w[...] = jnp.zeros_like(big_w)
    for e in range(ch):
        piece = wide[pl.ds(e, ch, stride=ch), :].astype(BF16)
        for g in range(groups):
            start = e * LANES + g * ch
            big_w[start : start + ch, g * pair_ch : (g + 1) * pair_ch] = piece

    for k in range(1, n_seq):
        other = (seq + k) % n_seq
        left_wait(col, other)
        for n in range(1, n_col):
            to_core(n, other).start()
    for n in range(1, n_col):
        for q in range(n_seq):
            left_wait((col + n) % n_col, q)

    def both_seqs(buf, at, rows):
        return jnp.concatenate([buf[(*at, q, rows)] for q in range(n_seq)], axis=1)

    def masks(buf, at, rows_to):
        found = [
            both_seqs(buf, (*at, n), slice(block, block + ROW_TILE)).astype(F32)[:res]
            for n in range(n_col)
        ]
        if rows_to > chip_res:
            found.append(jnp.zeros((rows_to - chip_res, n_seq * seqs), F32))
        return jnp.concatenate(found, axis=0).astype(BF16)

    left = jnp.concatenate(
        [both_seqs(left_buf, (n,), slice(0, block)) for n in range(n_col)], axis=0
    )
    left_mask = masks(left_buf, (), LANES)
    half_rows = ig_count * chip_res

    for piece in range(chunks):
        outers = []
        for n in range(n_col):
            for q in range(n_seq):
                pltpu.make_async_copy(
                    own_right, right_buf.at[piece, n, q], recv_right.at[piece, n, q]
                ).wait()
            outers.append(dot_nt(both_seqs(right_buf, (piece, n), slice(0, block)), left))
        for e in range(ch):
            both = jnp.concatenate([o[e * res : (e + 1) * res, :] for o in outers], axis=0)
            high = both.astype(BF16)
            low = (both - high.astype(F32)).astype(BF16)
            for ig in range(ig_count):
                rows = slice(ig * chip_res, (ig + 1) * chip_res)
                low_rows = slice(half_rows + ig * chip_res, half_rows + (ig + 1) * chip_res)
                lanes = slice(e * LANES, (e + 1) * LANES)
                spread[rows, lanes] = high[:, ig * LANES : (ig + 1) * LANES]
                spread[low_rows, lanes] = low[:, ig * LANES : (ig + 1) * LANES]
        product = jnp.dot(spread[...], big_w[...], preferred_element_type=F32)
        product = product[:half_rows] + product[half_rows:]
        counts = dot_nt(masks(right_buf, (piece,), chip_res), left_mask)
        scale = 1.0 / (counts + 0.001)
        place = slice(piece * chip_res, (piece + 1) * chip_res)
        for i in range(rows_i):
            ig, g = i // groups, i % groups
            update = product[
                ig * chip_res : (ig + 1) * chip_res, g * pair_ch : (g + 1) * pair_ch
            ]
            out_ref[i, place, :] = (
                pair_ref[i, place, :].astype(F32) + update * scale[:, i : i + 1]
            ).astype(BF16)

    for k in range(1, n_row):
        right_copy(k).wait_send()

    @pl.when(jnp.logical_not(stays))
    def _():
        right_copy(0).wait_send()

    for k in range(1, n_seq):
        to_seq(k).wait_send()
    for n in range(1, n_col):
        for q in range(n_seq):
            to_core(n, q).wait_send()


def on_device(
    sizes,
    alignment, alignment_mask, norm_gain, norm_bias, left_weight, left_bias, right_weight,
    right_bias, out_weight, pair_state,
):
    n_row, n_col, n_seq = sizes
    seqs, res, chans = alignment.shape
    ch = left_weight.shape[1]
    rows_i, cols_j, pair_ch = pair_state.shape
    block = res * ch + ROW_TILE
    chunks = cols_j // (res * n_col)
    groups = LANES // ch
    dma = pltpu.SemaphoreType.DMA
    return pl.pallas_call(
        functools.partial(kernel, sizes),
        out_shape=jax.ShapeDtypeStruct(pair_state.shape, BF16),
        in_specs=[pl.BlockSpec(memory_space=pl.ANY)] * 10,
        out_specs=pl.BlockSpec(memory_space=pltpu.VMEM),
        scratch_shapes=[
            pltpu.VMEM(alignment.shape, BF16),
            pltpu.VMEM((res, seqs), BF16),
            pltpu.VMEM((1, chans), F32),
            pltpu.VMEM((1, chans), F32),
            pltpu.VMEM((2 * ch, chans), BF16),
            pltpu.VMEM((1, ch), F32),
            pltpu.VMEM((1, ch), F32),
            pltpu.VMEM(out_weight.shape, BF16),
            pltpu.VMEM(pair_state.shape, BF16),
            pltpu.VMEM((chans // LANES, seqs * res, LANES), F32),
            pltpu.VMEM((res * ch, seqs), F32),
            pltpu.VMEM(out_weight.shape, F32),
            pltpu.VMEM((block, seqs), BF16),
            pltpu.VMEM((n_col, n_seq, block, seqs), BF16),
            pltpu.VMEM((chunks, n_col, n_seq, block, seqs), BF16),
            pltpu.VMEM((2 * (rows_i // groups) * res * n_col, ch * LANES), BF16),
            pltpu.VMEM((ch * LANES, groups * pair_ch), BF16),
            dma((9 + X_PARTS,)), dma((n_col, n_seq)), dma((n_col, n_seq)), dma((n_row,)),
            dma((chunks, n_col, n_seq)), dma((n_seq,)),
        ],
        compiler_params=pltpu.CompilerParams(
            collective_id=0, has_side_effects=True, vmem_limit_bytes=56 * 1024 * 1024
        ),
    )(
        alignment, alignment_mask.T, norm_gain.reshape(1, chans), norm_bias.reshape(1, chans),
        left_weight.T, left_bias.reshape(1, ch), right_weight.T, right_bias.reshape(1, ch),
        out_weight, pair_state,
    )


def solution(mesh):
    sizes = tuple(mesh.shape[name] for name in ("row", "col", "seq"))
    in_specs = (
        P(("groups", "seq"), ("row", "col"), None),
        P(("groups", "seq"), ("row", "col")),
        P(), P(), P(), P(), P(), P(), P(),
        P(("groups", "row"), ("col", "seq"), None),
    )
    return jax.shard_map(
        functools.partial(on_device, sizes),
        mesh=mesh,
        in_specs=in_specs,
        out_specs=P(("groups", "row"), ("col", "seq"), None),
        check_vma=False,
    )
```

```python
import functools

import jax
import jax.numpy as jnp
from jax import lax
from jax.experimental import pallas as pl
from jax.experimental.pallas import tpu as pltpu
from jax.sharding import PartitionSpec as P

MESH = pl.DeviceIdType.MESH
F32 = jnp.float32
BF16 = jnp.bfloat16
ROW_TILE = 16
LANES = 128
X_PARTS = 4


def dot_nt(a, b):
    return lax.dot_general(a, b, (((1,), (1,)), ((), ())), preferred_element_type=F32)


def kernel(
    sizes,
    x_hbm, mask_hbm, gain_hbm, bias_hbm, wl_hbm, bl_hbm, wr_hbm, br_hbm, wout_hbm, pair_hbm,
    out_ref,
    x_ref, mask_ref, gain_ref, bias_ref, weight_ref, bl_ref, br_ref, wout_ref, pair_ref,
    normed, shuffle, wide, own_right, left_buf, right_buf, spread, big_w,
    in_sem, send_left, recv_left, send_right, recv_right, send_seq, ready,
):
    n_row, n_col, n_seq = sizes
    seqs, res, chans = x_ref.shape
    ch = wl_hbm.shape[0]
    rows_i, cols_j, pair_ch = pair_ref.shape
    block = res * ch
    chip_res = res * n_col
    chunks = cols_j // chip_res
    cores = n_col * n_seq
    groups = LANES // ch
    ig_count = rows_i // groups
    row, col, seq = lax.axis_index("row"), lax.axis_index("col"), lax.axis_index("seq")
    here = col * n_seq + seq
    dest_col, dest_seq = row // chunks // n_seq, row // chunks % n_seq
    stays = dest_col * n_seq + dest_seq == here
    my_chunk = row % chunks
    in_turn = row == n_row - 1

    copies = [
        pltpu.make_async_copy(mask_hbm, mask_ref, in_sem.at[0]),
        pltpu.make_async_copy(gain_hbm, gain_ref, in_sem.at[1]),
        pltpu.make_async_copy(bias_hbm, bias_ref, in_sem.at[2]),
        pltpu.make_async_copy(wl_hbm, weight_ref.at[0:ch], in_sem.at[3]),
        pltpu.make_async_copy(wr_hbm, weight_ref.at[ch : 2 * ch], in_sem.at[4]),
        pltpu.make_async_copy(bl_hbm, bl_ref, in_sem.at[5]),
        pltpu.make_async_copy(br_hbm, br_ref, in_sem.at[6]),
    ]
    late = [
        pltpu.make_async_copy(wout_hbm, wout_ref, in_sem.at[7]),
        pltpu.make_async_copy(pair_hbm, pair_ref, in_sem.at[8]),
    ]
    part = seqs // X_PARTS
    x_copies = [
        pltpu.make_async_copy(
            x_hbm.at[n * part : (n + 1) * part], x_ref.at[n * part : (n + 1) * part],
            in_sem.at[9 + n],
        )
        for n in range(X_PARTS)
    ]
    for copy in x_copies:
        copy.start()

    barrier = pltpu.get_barrier_semaphore()
    for piece in range(chunks):
        source = here * chunks + piece
        for n in range(cores):
            @pl.when((source > row) | ((source == row) & (here != n)))
            def _():
                pl.semaphore_signal(
                    barrier, inc=1, device_id_type=MESH,
                    device_id={"row": source, "col": n // n_seq, "seq": n % n_seq},
                )
    for to_row in range(1, n_row):
        @pl.when(to_row > row)
        def _():
            pl.semaphore_signal(
                barrier, inc=1, device_id_type=MESH,
                device_id={"row": to_row, "col": dest_col, "seq": dest_seq},
            )
    near = n_col - 1 + n_seq - 1
    for n in range(1, n_col):
        pl.semaphore_signal(
            barrier, inc=1, device_id={"col": (col + n) % n_col}, device_id_type=MESH
        )
    for k in range(1, n_seq):
        pl.semaphore_signal(
            barrier, inc=1, device_id={"seq": (seq + k) % n_seq}, device_id_type=MESH
        )

    for copy in copies + late:
        copy.start()
    lower_sources = jnp.clip(row - here * chunks, 0, chunks)
    pl.semaphore_wait(barrier, near + row + jnp.where(stays, 0, 1) + cores * lower_sources)
    for piece in range(chunks):
        source = here * chunks + piece
        for n in range(cores):
            @pl.when(source < row)
            def _():
                pl.semaphore_signal(
                    ready.at[row], inc=1, device_id_type=MESH,
                    device_id={"row": source, "col": n // n_seq, "seq": n % n_seq},
                )

    for copy in copies:
        copy.wait()
    gain, shift = gain_ref[...], bias_ref[...]
    step = 16
    for first in range(0, seqs, step):
        if first % part == 0:
            x_copies[first // part].wait()
        values = x_ref[first : first + step].astype(F32).reshape(step * res, chans)
        center = jnp.mean(values, axis=-1, keepdims=True)
        values = values - center
        var = jnp.mean(values * values, axis=-1, keepdims=True)
        values = values * lax.rsqrt(var + 1e-05) * gain + shift
        for lane in range(0, chans, LANES):
            normed[lane // LANES, first * res : (first + step) * res, :] = values[
                :, lane : lane + LANES
            ]

    weight_t = weight_ref[...]
    bias_t = jnp.concatenate([bl_ref[...], br_ref[...]], axis=1)
    bias_t = jnp.broadcast_to(bias_t, (8, 2 * ch)).T[:, 0:1]
    mask_t = mask_ref[...].astype(F32)
    for r in range(res):
        picked = jnp.concatenate(
            [normed[h, pl.ds(r, seqs, stride=res), :] for h in range(chans // LANES)], axis=1
        ).astype(BF16)
        proj = (dot_nt(weight_t, picked) + bias_t) * mask_t[r : r + 1, :]
        left_buf[col, seq, r * ch : (r + 1) * ch, :] = proj[:ch].astype(BF16)
        shuffle[pl.ds(r, ch, stride=res), :] = proj[ch:]
    mask_rows = jnp.concatenate([mask_t, jnp.zeros_like(mask_t)], axis=0)[:ROW_TILE].astype(BF16)
    left_buf[col, seq, block : block + ROW_TILE, :] = mask_rows
    own_right[0:block, :] = shuffle[...].astype(BF16)
    own_right[block : block + ROW_TILE, :] = mask_rows

    def to_seq(k):
        return pltpu.make_async_remote_copy(
            src_ref=left_buf.at[col, seq], dst_ref=left_buf.at[col, seq],
            send_sem=send_seq.at[k], recv_sem=recv_left.at[col, seq],
            device_id={"seq": (seq + k) % n_seq}, device_id_type=MESH,
        )

    def to_core(n, q):
        return pltpu.make_async_remote_copy(
            src_ref=left_buf.at[col, q], dst_ref=left_buf.at[col, q],
            send_sem=send_left.at[n, q], recv_sem=recv_left.at[col, q],
            device_id={"col": (col + n) % n_col}, device_id_type=MESH,
        )

    def left_wait(n, q):
        pltpu.make_async_copy(own_right, left_buf.at[n, q], recv_left.at[n, q]).wait()

    def right_copy(k):
        to_row = row if k == 0 else lax.select(k - 1 < row, k - 1, k)
        if k > 0:
            to_row = lax.select(row == n_row - 1, n_row - 1 - k, to_row)
        return pltpu.make_async_remote_copy(
            src_ref=own_right, dst_ref=right_buf.at[my_chunk, col, seq],
            send_sem=send_right.at[k], recv_sem=recv_right.at[my_chunk, col, seq],
            device_id={"row": to_row, "col": dest_col, "seq": dest_seq},
            device_id_type=MESH,
        )

    def right_local():
        return pltpu.make_async_copy(
            own_right, right_buf.at[my_chunk, col, seq], recv_right.at[my_chunk, col, seq]
        )

    for n in range(1, n_col):
        to_core(n, seq).start()
    for k in range(1, n_seq):
        to_seq(k).start()
    @pl.when(stays)
    def _():
        right_local().start()

    @pl.when(jnp.logical_not(stays))
    def _():
        right_copy(0).start()

    for k in range(1, n_row):
        @pl.when(k > row)
        def _():
            pl.semaphore_wait(ready.at[k], 1)

        if k == 2:
            pl.when(in_turn)(right_copy(1).wait_send)
        right_copy(k).start()

    for copy in late:
        copy.wait()
    wide[...] = wout_ref[...].astype(F32)
    big_w[...] = jnp.zeros_like(big_w)
    for e in range(ch):
        piece = wide[pl.ds(e, ch, stride=ch), :].astype(BF16)
        for g in range(groups):
            start = e * LANES + g * ch
            big_w[start : start + ch, g * pair_ch : (g + 1) * pair_ch] = piece

    for k in range(1, n_seq):
        other = (seq + k) % n_seq
        left_wait(col, other)
        for n in range(1, n_col):
            to_core(n, other).start()
    for n in range(1, n_col):
        for q in range(n_seq):
            left_wait((col + n) % n_col, q)

    def both_seqs(buf, at, rows):
        return jnp.concatenate([buf[(*at, q, rows)] for q in range(n_seq)], axis=1)

    def masks(buf, at, rows_to):
        found = [
            both_seqs(buf, (*at, n), slice(block, block + ROW_TILE)).astype(F32)[:res]
            for n in range(n_col)
        ]
        if rows_to > chip_res:
            found.append(jnp.zeros((rows_to - chip_res, n_seq * seqs), F32))
        return jnp.concatenate(found, axis=0).astype(BF16)

    left = jnp.concatenate(
        [both_seqs(left_buf, (n,), slice(0, block)) for n in range(n_col)], axis=0
    )
    left_mask = masks(left_buf, (), LANES)
    half_rows = ig_count * chip_res

    for piece in range(chunks):
        outers = []
        for n in range(n_col):
            for q in range(n_seq):
                pltpu.make_async_copy(
                    own_right, right_buf.at[piece, n, q], recv_right.at[piece, n, q]
                ).wait()
            outers.append(dot_nt(both_seqs(right_buf, (piece, n), slice(0, block)), left))
        for e in range(ch):
            both = jnp.concatenate([o[e * res : (e + 1) * res, :] for o in outers], axis=0)
            high = both.astype(BF16)
            low = (both - high.astype(F32)).astype(BF16)
            for ig in range(ig_count):
                rows = slice(ig * chip_res, (ig + 1) * chip_res)
                low_rows = slice(half_rows + ig * chip_res, half_rows + (ig + 1) * chip_res)
                lanes = slice(e * LANES, (e + 1) * LANES)
                spread[rows, lanes] = high[:, ig * LANES : (ig + 1) * LANES]
                spread[low_rows, lanes] = low[:, ig * LANES : (ig + 1) * LANES]
        product = jnp.dot(spread[...], big_w[...], preferred_element_type=F32)
        product = product[:half_rows] + product[half_rows:]
        counts = dot_nt(masks(right_buf, (piece,), chip_res), left_mask)
        scale = 1.0 / (counts + 0.001)
        place = slice(piece * chip_res, (piece + 1) * chip_res)
        for i in range(rows_i):
            ig, g = i // groups, i % groups
            update = product[
                ig * chip_res : (ig + 1) * chip_res, g * pair_ch : (g + 1) * pair_ch
            ]
            out_ref[i, place, :] = (
                pair_ref[i, place, :].astype(F32) + update * scale[:, i : i + 1]
            ).astype(BF16)

    pl.when(jnp.logical_not(in_turn))(right_copy(1).wait_send)
    for k in range(2, n_row):
        right_copy(k).wait_send()

    @pl.when(jnp.logical_not(stays))
    def _():
        right_copy(0).wait_send()

    for k in range(1, n_seq):
        to_seq(k).wait_send()
    for n in range(1, n_col):
        for q in range(n_seq):
            to_core(n, q).wait_send()


def on_device(
    sizes,
    alignment, alignment_mask, norm_gain, norm_bias, left_weight, left_bias, right_weight,
    right_bias, out_weight, pair_state,
):
    n_row, n_col, n_seq = sizes
    seqs, res, chans = alignment.shape
    ch = left_weight.shape[1]
    rows_i, cols_j, pair_ch = pair_state.shape
    block = res * ch + ROW_TILE
    chunks = cols_j // (res * n_col)
    groups = LANES // ch
    dma = pltpu.SemaphoreType.DMA
    return pl.pallas_call(
        functools.partial(kernel, sizes),
        out_shape=jax.ShapeDtypeStruct(pair_state.shape, BF16),
        in_specs=[pl.BlockSpec(memory_space=pl.ANY)] * 10,
        out_specs=pl.BlockSpec(memory_space=pltpu.VMEM),
        scratch_shapes=[
            pltpu.VMEM(alignment.shape, BF16),
            pltpu.VMEM((res, seqs), BF16),
            pltpu.VMEM((1, chans), F32),
            pltpu.VMEM((1, chans), F32),
            pltpu.VMEM((2 * ch, chans), BF16),
            pltpu.VMEM((1, ch), F32),
            pltpu.VMEM((1, ch), F32),
            pltpu.VMEM(out_weight.shape, BF16),
            pltpu.VMEM(pair_state.shape, BF16),
            pltpu.VMEM((chans // LANES, seqs * res, LANES), F32),
            pltpu.VMEM((res * ch, seqs), F32),
            pltpu.VMEM(out_weight.shape, F32),
            pltpu.VMEM((block, seqs), BF16),
            pltpu.VMEM((n_col, n_seq, block, seqs), BF16),
            pltpu.VMEM((chunks, n_col, n_seq, block, seqs), BF16),
            pltpu.VMEM((2 * (rows_i // groups) * res * n_col, ch * LANES), BF16),
            pltpu.VMEM((ch * LANES, groups * pair_ch), BF16),
            dma((9 + X_PARTS,)), dma((n_col, n_seq)), dma((n_col, n_seq)), dma((n_row,)),
            dma((chunks, n_col, n_seq)), dma((n_seq,)),
            pltpu.SemaphoreType.REGULAR((n_row,)),
        ],
        compiler_params=pltpu.CompilerParams(
            collective_id=0, has_side_effects=True, vmem_limit_bytes=56 * 1024 * 1024
        ),
    )(
        alignment, alignment_mask.T, norm_gain.reshape(1, chans), norm_bias.reshape(1, chans),
        left_weight.T, left_bias.reshape(1, ch), right_weight.T, right_bias.reshape(1, ch),
        out_weight, pair_state,
    )


def solution(mesh):
    sizes = tuple(mesh.shape[name] for name in ("row", "col", "seq"))
    in_specs = (
        P(("groups", "seq"), ("row", "col"), None),
        P(("groups", "seq"), ("row", "col")),
        P(), P(), P(), P(), P(), P(), P(),
        P(("groups", "row"), ("col", "seq"), None),
    )
    return jax.shard_map(
        functools.partial(on_device, sizes),
        mesh=mesh,
        in_specs=in_specs,
        out_specs=P(("groups", "row"), ("col", "seq"), None),
        check_vma=False,
    )
```
